128 devices in a mesh: feat: 32 (over z, x_lo, y), tok: 4 (over x_hi, core).
Axes of the slice: x: 4 (x_hi: 2, x_lo: 2; x = x_hi * 2 + x_lo), y: 4, z: 4, core: 2. Of those that a mesh axis runs over, the one named last changes fastest.
Arguments:
- activations: bfloat16 [3072, 8192], P('tok', 'feat'), may hold values from -6 to 6
- up_weight: bfloat16 [256, 6, 256, 256], P('feat'), may hold values from -0.15625 to 0.15625
- down_weight: bfloat16 [256, 6, 256, 256], P('feat'), may hold values from -0.0546875 to 0.0546875
- out_grad: bfloat16 [3072, 8192], P('tok', 'feat'), may hold values from -6 to 6
Outputs:
- output: bfloat16 [3072, 8192], P('tok', 'feat')
- in_grad: bfloat16 [3072, 8192], P('tok', 'feat')
- up_grad: float32 [256, 6, 256, 256], P(('feat', 'tok'))
- down_grad: float32 [256, 6, 256, 256], P(('feat', 'tok'))
The draws below stay inside these ranges and needn't reach their ends.
All inputs are finite; a program needn't handle non-finite values.
Results may differ from the reference program's by a relative error of at most 0.012.
Values may be sent and summed in bfloat16 or wider, within the bound.
No kernel may reach another device: no remote copies, remote signals or barrier semaphores. Data moves between devices by JAX's collectives and lax.ppermute only.
A program may use at most 128 MiB of HBM per device.

```python
import jax
import jax.numpy as jnp
import numpy as np
from jax import lax

BLOCK = 256
HB_DEV = 8
TOK_DEV = 768
LEVELS = 5
SLOTS = 6
D = 8192
H_BLOCKS = 256
TOKENS = 3072
N_FEAT = 32
N_TOK = 4


def levels(own_key, extent, cuts, low, top_value):
    def one(position, parts):
        heights = jax.random.uniform(jax.random.fold_in(jax.random.fold_in(own_key, 6), position), (parts,), jnp.float32, low / len(cuts), top_value / len(cuts))
        return jnp.repeat(jnp.exp(heights), extent[position] // parts).reshape((-1,) + (1,) * (len(extent) - position - 1))

    factor_of = one(*cuts[0])
    for cut in cuts[1:]:
        factor_of = factor_of * one(*cut)
    return factor_of


def gaussian(stream_key, shape, scale, bound, split=(), kind=jnp.bfloat16):
    drawn = jax.random.normal(stream_key, shape, jnp.float32) * scale
    if len(split) > 0:
        drawn = levels(stream_key, shape, split, -0.22, 0.18) * drawn
    return jnp.clip(drawn, min=-bound, max=bound).astype(kind)


def setup_inputs(seed: int = 0) -> dict:
    arg_keys = jax.random.split(jax.random.key(seed), 5)
    return {
        "activations": gaussian(arg_keys[0], (TOKENS, D), 1.0, 6.0, ((0, 4), (1, 32))),
        "up_weight": gaussian(arg_keys[1], (H_BLOCKS, SLOTS, BLOCK, BLOCK), (SLOTS * BLOCK) ** -0.5, 0.15625, ((0, 32),)),
        "down_weight": gaussian(arg_keys[2], (H_BLOCKS, SLOTS, BLOCK, BLOCK), (SLOTS * HB_DEV * BLOCK) ** -0.5, 0.0546875, ((0, 32),)),
        "out_grad": gaussian(arg_keys[3], (TOKENS, D), 1.0, 6.0, ((0, 4), (1, 32))),
    }


tanh_scale = 0.7978845608028654


def gelu_terms(values):
    inner = tanh_scale * (values + 0.044715 * values * values * values)
    tangent = jnp.tanh(inner)
    result = 0.5 * values * (1.0 + tangent)
    derivative = 0.5 * (1.0 + tangent) + 0.5 * values * (1.0 - tangent * tangent) * tanh_scale * (1.0 + 3.0 * 0.044715 * values * values)
    return result, derivative


def partner_table():
    rows = [[index] + [index ^ (1 << level) for level in range(LEVELS)] for index in range(N_FEAT)]
    return np.array(rows, np.int32)


def reference(activations, up_weight, down_weight, out_grad):
    table = jnp.asarray(partner_table(), jnp.int32)
    act_blocks = activations.reshape(TOKENS, N_FEAT, BLOCK)
    grad_blocks = out_grad.reshape(TOKENS, N_FEAT, BLOCK)
    up_groups = up_weight.reshape(N_FEAT, HB_DEV, SLOTS, BLOCK, BLOCK)
    down_groups = down_weight.reshape(N_FEAT, HB_DEV, SLOTS, BLOCK, BLOCK)

    def per_group(carry, group):
        out_acc, in_acc = carry
        partners = table[group]
        act_near = jnp.take(act_blocks, partners, axis=1).astype(jnp.float32)
        grad_near = jnp.take(grad_blocks, partners, axis=1).astype(jnp.float32)
        up_here = up_groups[group].astype(jnp.float32)
        down_here = down_groups[group].astype(jnp.float32)
        pre_act = jnp.einsum('tsb,jsbc->tjc', act_near, up_here)
        result, derivative = gelu_terms(pre_act)
        hidden = result.astype(jnp.bfloat16).astype(jnp.float32)
        out_parts = jnp.einsum('tjb,jsbc->tsc', hidden, down_here)
        hidden_grad = jnp.einsum('tsc,jsbc->tjb', grad_near, down_here)
        pre_grad = (hidden_grad * derivative).astype(jnp.bfloat16).astype(jnp.float32)
        in_parts = jnp.einsum('tjc,jsbc->tsb', pre_grad, up_here)
        out_acc = out_acc.at[:, partners].add(out_parts)
        in_acc = in_acc.at[:, partners].add(in_parts)
        act_split = act_near.reshape(N_TOK, TOK_DEV, SLOTS, BLOCK)
        grad_split = grad_near.reshape(N_TOK, TOK_DEV, SLOTS, BLOCK)
        hidden_split = hidden.reshape(N_TOK, TOK_DEV, HB_DEV, BLOCK)
        pre_split = pre_grad.reshape(N_TOK, TOK_DEV, HB_DEV, BLOCK)
        up_terms = jnp.einsum('ntsb,ntjc->njsbc', act_split, pre_split).astype(jnp.bfloat16)
        up_terms = lax.optimization_barrier(up_terms).astype(jnp.float32)
        down_terms = jnp.einsum('ntjb,ntsc->njsbc', hidden_split, grad_split).astype(jnp.bfloat16)
        down_terms = lax.optimization_barrier(down_terms).astype(jnp.float32)
        return (out_acc, in_acc), (jnp.sum(up_terms, axis=0), jnp.sum(down_terms, axis=0))

    start = (jnp.zeros((TOKENS, N_FEAT, BLOCK), jnp.float32), jnp.zeros((TOKENS, N_FEAT, BLOCK), jnp.float32))
    (out_acc, in_acc), (up_all, down_all) = lax.scan(per_group, start, jnp.arange(N_FEAT, dtype=jnp.int32))
    output = out_acc.reshape(TOKENS, D).astype(jnp.bfloat16)
    in_grad = in_acc.reshape(TOKENS, D).astype(jnp.bfloat16)
    up_grad = up_all.reshape(H_BLOCKS, SLOTS, BLOCK, BLOCK)
    down_grad = down_all.reshape(H_BLOCKS, SLOTS, BLOCK, BLOCK)
    return (output, in_grad, up_grad, down_grad)
```

```python
import jax
import jax.numpy as jnp
from jax import lax
from jax.experimental import pallas as pl
from jax.experimental.pallas import tpu as pltpu
from jax.sharding import PartitionSpec as P

F32 = jnp.float32
BF = jnp.bfloat16
TANH_SCALE = 0.7978845608028654
BLOCK = 256
SLOTS = 6
HELD = 4
ROWS = 768

CORE, X2, X1, X3, Y1, Y3, Z1, Z3 = 1, 2, 16, 18, 4, 12, 32, 96

ANY = pl.BlockSpec(memory_space=pl.ANY)
VMEM = pl.BlockSpec(memory_space=pltpu.VMEM)
SMEM = pl.BlockSpec(memory_space=pltpu.SMEM)
NT = (((1,), (1,)), ((), ()))
TN = (((0,), (0,)), ((), ()))


def swapped(array, mask):
    count = lax.axis_size("feat") * lax.axis_size("tok")
    return lax.ppermute(array, ("feat", "tok"), [(i, i ^ mask) for i in range(count)])


def gelu_terms(values):
    square = values * values
    half = 0.5 + 0.5 * jnp.tanh(TANH_SCALE * (values + 0.044715 * (square * values)))
    slope = TANH_SCALE + (3.0 * 0.044715 * TANH_SCALE) * square
    return values * half, half + (2.0 * values) * (half * (1.0 - half)) * slope


def matmul(a, b, dims=(((1,), (0,)), ((), ()))):
    return lax.dot_general(a, b, dims, preferred_element_type=F32)


def total(parts):
    result = None
    for part in parts:
        result = part if result is None else result + part
    return result


def columns(j):
    return pl.ds(j * BLOCK, BLOCK)


def call(body, name, operands, outs, matmuls, specs=None, scratch=()):
    return pl.pallas_call(
        body,
        in_specs=specs or [VMEM] * len(operands),
        out_specs=[VMEM] * len(outs),
        out_shape=[jax.ShapeDtypeStruct(shape, kind) for shape, kind in outs],
        scratch_shapes=list(scratch),
        compiler_params=pltpu.CompilerParams(vmem_limit_bytes=24 << 20),
        cost_estimate=pl.CostEstimate(
            flops=matmuls * 2 * ROWS * BLOCK * BLOCK, bytes_accessed=1 << 20, transcendentals=0
        ),
        name=name,
    )(*operands)


def take_weights(half, up_weight, down_weight):
    def body(half_ref, up_ref, down_ref, up_out, down_out, sems):
        held = pl.ds(half_ref[0] * HELD, HELD)
        up = pltpu.make_async_copy(up_ref.at[held], up_out, sems.at[0])
        down = pltpu.make_async_copy(down_ref.at[held], down_out, sems.at[1])
        up.start()
        down.start()
        up.wait()
        down.wait()

    shape = ((HELD, SLOTS, BLOCK, BLOCK), BF)
    return call(
        body, "take_weights", (half, up_weight, down_weight), [shape, shape], 8,
        specs=[SMEM, ANY, ANY], scratch=[pltpu.SemaphoreType.DMA((2,))],
    )


def forward(near, up, down):
    def body(*refs):
        near_refs, (up_ref, down_ref, hidden, derivative), outs = (
            refs[:SLOTS], refs[SLOTS:SLOTS + 4], refs[SLOTS + 4:]
        )
        for j in range(HELD):
            pre_act = total(matmul(near_refs[s][...], up_ref[j, s]) for s in range(SLOTS))
            result, slope = gelu_terms(pre_act)
            hidden[:, columns(j)] = result.astype(BF)
            derivative[:, columns(j)] = slope.astype(BF)
        for s in range(SLOTS):
            outs[s][...] = total(
                matmul(hidden[:, columns(j)], down_ref[j, s]) for j in range(HELD)
            ).astype(BF)

    wide, part = ((ROWS, HELD * BLOCK), BF), ((ROWS, BLOCK), BF)
    hidden, derivative, *parts = call(
        body, "forward", (*near, up, down), [wide, wide] + [part] * SLOTS, 2 * HELD * SLOTS
    )
    return hidden, derivative, parts


def backward(near, derivative, up, down):
    def body(*refs):
        near_refs, (slope, up_ref, down_ref, pre_grad), outs = (
            refs[:SLOTS], refs[SLOTS:SLOTS + 4], refs[SLOTS + 4:]
        )
        for j in range(HELD):
            hidden_grad = total(matmul(near_refs[s][...], down_ref[j, s], NT) for s in range(SLOTS))
            pre_grad[:, columns(j)] = (hidden_grad * slope[:, columns(j)].astype(F32)).astype(BF)
        for s in range(SLOTS):
            outs[s][...] = total(
                matmul(pre_grad[:, columns(j)], up_ref[j, s], NT) for j in range(HELD)
            ).astype(BF)

    wide, part = ((ROWS, HELD * BLOCK), BF), ((ROWS, BLOCK), BF)
    pre_grad, *parts = call(
        body, "backward", (*near, derivative, up, down), [wide] + [part] * SLOTS, 2 * HELD * SLOTS
    )
    return pre_grad, parts


def up_weight_grad(core, own, other, pre_grad, pre_grad_other):
    def body(core_ref, *refs):
        own_refs, other_refs, (grad, grad_other, keep, send) = (
            refs[:SLOTS], refs[SLOTS:2 * SLOTS], refs[2 * SLOTS:]
        )
        for mine, out in ((0, send), (1, keep)):
            group = jnp.where(core_ref[0] == mine, 1, 0)
            wide = pl.ds(pl.multiple_of(group * (2 * BLOCK), 2 * BLOCK), 2 * BLOCK)
            for s in range(SLOTS):
                result = matmul(own_refs[s][...], grad[:, wide], TN)
                result += matmul(other_refs[s][...], grad_other[:, wide], TN)
                for i in range(2):
                    out[i, s] = result[:, i * BLOCK:(i + 1) * BLOCK].astype(BF)

    shape = ((2, SLOTS, BLOCK, BLOCK), BF)
    return call(
        body, "up_weight_grad", (core, *own, *other, pre_grad, pre_grad_other), [shape, shape],
        2 * HELD * SLOTS, specs=[SMEM] + [VMEM] * (2 * SLOTS + 2),
    )


def down_weight_grad(core, own, other, hidden, hidden_other):
    def body(core_ref, *refs):
        own_refs, other_refs, (act, act_other, keep, send) = (
            refs[:SLOTS], refs[SLOTS:2 * SLOTS], refs[2 * SLOTS:]
        )
        for mine, out in ((0, send), (1, keep)):
            group = jnp.where(core_ref[0] == mine, 1, 0)
            wide = pl.ds(pl.multiple_of(group * (2 * BLOCK), 2 * BLOCK), 2 * BLOCK)
            for s in range(SLOTS):
                result = matmul(act[:, wide], own_refs[s][...], TN)
                result += matmul(act_other[:, wide], other_refs[s][...], TN)
                for i in range(2):
                    out[i, s] = result[i * BLOCK:(i + 1) * BLOCK].astype(BF)

    shape = ((2, SLOTS, BLOCK, BLOCK), BF)
    return call(
        body, "down_weight_grad", (core, *own, *other, hidden, hidden_other), [shape, shape],
        2 * HELD * SLOTS, specs=[SMEM] + [VMEM] * (2 * SLOTS + 2),
    )


def added(*arrays):
    return total(a.astype(F32) for a in arrays).astype(BF)


def per_device(activations, up_weight, down_weight, out_grad):
    place = lax.axis_index("tok")
    half = (place // 2).astype(jnp.int32).reshape(1)
    core = (place % 2).astype(jnp.int32).reshape(1)

    def spread(own):
        y1, z1, x1 = swapped(own, Y1), swapped(own, Z1), swapped(own, X1)
        y2, z2 = swapped(y1, Y3), swapped(z1, Z3)
        far, x3 = swapped(own, X2), swapped(own, X3)
        far_y1, far_z1 = swapped(far, Y1), swapped(far, Z1)
        far_y2, far_z2 = swapped(far_y1, Y3), swapped(far_z1, Z3)
        return [own, y1, y2, x1, z1, z2], [far, far_y1, far_y2, x3, far_z1, far_z2]

    def gathered(parts):
        y = swapped(added(swapped(parts[2], Y3), parts[1]), Y1)
        z = swapped(added(swapped(parts[5], Z3), parts[4]), Z1)
        return parts[0], y, z

    def collected(parts, far_parts):
        far = swapped(added(*gathered(far_parts)), X2)
        return added(*gathered(parts), swapped(parts[3], X1), swapped(far_parts[3], X3), far)

    act_near, act_far = spread(activations)
    grad_near, grad_far = spread(out_grad)
    up, down = take_weights(half, up_weight, down_weight)
    hidden, slope, out_parts = forward(act_near, up, down)
    hidden_far, slope_far, out_far = forward(act_far, up, down)
    pre_grad, in_parts = backward(grad_near, slope, up, down)
    pre_grad_far, in_far = backward(grad_far, slope_far, up, down)
    output = collected(out_parts, out_far)
    in_grad = collected(in_parts, in_far)
    down_keep, down_send = down_weight_grad(core, grad_near, grad_far, hidden, hidden_far)
    up_keep, up_send = up_weight_grad(core, act_near, act_far, pre_grad, pre_grad_far)
    up_grad = up_keep.astype(F32) + swapped(up_send, CORE).astype(F32)
    down_grad = down_keep.astype(F32) + swapped(down_send, CORE).astype(F32)
    return output, in_grad, up_grad, down_grad


def solution(mesh):
    in_specs = (
        P("tok", "feat"),
        P("feat", None, None, None),
        P("feat", None, None, None),
        P("tok", "feat"),
    )
    out_specs = (
        P("tok", "feat"),
        P("tok", "feat"),
        P(("feat", "tok"), None, None, None),
        P(("feat", "tok"), None, None, None),
    )
    return jax.shard_map(
        per_device, mesh=mesh, in_specs=in_specs, out_specs=out_specs, check_vma=False
    )
```

```python
import jax
import jax.numpy as jnp
from jax import lax
from jax.experimental import pallas as pl
from jax.experimental.pallas import tpu as pltpu
from jax.sharding import PartitionSpec as P

F32 = jnp.float32
BF = jnp.bfloat16
TANH_SCALE = 0.7978845608028654
BLOCK = 256
SLOTS = 6
HELD = 8
ROWS = 768

CORE, X2, X1, X3, Y1, Y3, Z1, Z3 = 1, 2, 16, 18, 4, 12, 32, 96

VMEM = pl.BlockSpec(memory_space=pltpu.VMEM)
SMEM = pl.BlockSpec(memory_space=pltpu.SMEM)
NT = (((1,), (1,)), ((), ()))
TN = (((0,), (0,)), ((), ()))


def swapped(array, mask):
    count = lax.axis_size("feat") * lax.axis_size("tok")
    return lax.ppermute(array, ("feat", "tok"), [(i, i ^ mask) for i in range(count)])


def gelu_terms(values):
    square = values * values
    half = 0.5 + 0.5 * jnp.tanh(TANH_SCALE * (values + 0.044715 * (square * values)))
    slope = TANH_SCALE + (3.0 * 0.044715 * TANH_SCALE) * square
    return values * half, half + (2.0 * values) * (half * (1.0 - half)) * slope


def matmul(a, b, dims=(((1,), (0,)), ((), ()))):
    return lax.dot_general(a, b, dims, preferred_element_type=F32)


def total(parts):
    result = None
    for part in parts:
        result = part if result is None else result + part
    return result


def columns(j):
    return pl.ds(j * BLOCK, BLOCK)


def call(body, name, operands, outs, matmuls, specs=None, scratch=()):
    return pl.pallas_call(
        body,
        in_specs=specs or [VMEM] * len(operands),
        out_specs=[VMEM] * len(outs),
        out_shape=[jax.ShapeDtypeStruct(shape, kind) for shape, kind in outs],
        scratch_shapes=list(scratch),
        compiler_params=pltpu.CompilerParams(vmem_limit_bytes=24 << 20),
        cost_estimate=pl.CostEstimate(
            flops=matmuls * 2 * ROWS * BLOCK * BLOCK, bytes_accessed=1 << 20, transcendentals=0
        ),
        name=name,
    )(*operands)


WIDE = ((ROWS, HELD * BLOCK), BF)
PART = ((ROWS, BLOCK), BF)


def hidden_of(near, up):
    def body(*refs):
        near_refs, (up_ref, hidden, derivative) = refs[:SLOTS], refs[SLOTS:]
        for j in range(HELD):
            pre_act = total(matmul(near_refs[s][...], up_ref[j, s]) for s in range(SLOTS))
            result, slope = gelu_terms(pre_act)
            hidden[:, columns(j)] = result.astype(BF)
            derivative[:, columns(j)] = slope.astype(BF)

    return call(body, "hidden_of", (*near, up), [WIDE, WIDE], HELD * SLOTS)


def out_parts_of(hidden, down):
    def body(hidden_ref, down_ref, *outs):
        for s in range(SLOTS):
            outs[s][...] = total(
                matmul(hidden_ref[:, columns(j)], down_ref[j, s]) for j in range(HELD)
            ).astype(BF)

    return call(body, "out_parts_of", (hidden, down), [PART] * SLOTS, HELD * SLOTS)


def pre_grad_of(near, derivative, down):
    def body(*refs):
        near_refs, (slope, down_ref, pre_grad) = refs[:SLOTS], refs[SLOTS:]
        for j in range(HELD):
            hidden_grad = total(matmul(near_refs[s][...], down_ref[j, s], NT) for s in range(SLOTS))
            pre_grad[:, columns(j)] = (hidden_grad * slope[:, columns(j)].astype(F32)).astype(BF)

    return call(body, "pre_grad_of", (*near, derivative, down), [WIDE], HELD * SLOTS)[0]


def in_parts_of(pre_grad, up):
    def body(grad_ref, up_ref, *outs):
        for s in range(SLOTS):
            outs[s][...] = total(
                matmul(grad_ref[:, columns(j)], up_ref[j, s], NT) for j in range(HELD)
            ).astype(BF)

    return call(body, "in_parts_of", (pre_grad, up), [PART] * SLOTS, HELD * SLOTS)


def weight_grad(name, place, near, wide, hidden_first):
    def body(place_ref, *refs):
        near_refs, (wide_ref, keep, send) = refs[:SLOTS], refs[SLOTS:]
        for other, out in ((1, send), (0, keep)):
            core = jnp.where(place_ref[1] == other, 0, 1)
            first = (place_ref[0] * 2 + core) * (2 * BLOCK)
            chosen = pl.ds(pl.multiple_of(first, 2 * BLOCK), 2 * BLOCK)
            for s in range(SLOTS):
                if hidden_first:
                    result = matmul(wide_ref[:, chosen], near_refs[s][...], TN)
                else:
                    result = matmul(near_refs[s][...], wide_ref[:, chosen], TN)
                for i in range(2):
                    cut = slice(i * BLOCK, (i + 1) * BLOCK)
                    out[i, s] = (result[cut] if hidden_first else result[:, cut]).astype(BF)

    shape = ((2, SLOTS, BLOCK, BLOCK), BF)
    return call(
        body, name, (place, *near, wide), [shape, shape], HELD * SLOTS // 2,
        specs=[SMEM] + [VMEM] * (SLOTS + 1),
    )


def added(*arrays):
    return total(a.astype(F32) for a in arrays).astype(BF)


def after(array, *before):
    return lax.optimization_barrier((array, *before))[0]


def send(array, mask, *before):
    return swapped(after(array, *before) if before else array, mask)


def per_device(activations, up_weight, down_weight, out_grad):
    tok = lax.axis_index("tok").astype(jnp.int32)
    x_hi, core = tok // 2, tok % 2
    own_chip, far_chip = jnp.stack([x_hi, core]), jnp.stack([1 - x_hi, core])

    act, grad = [activations] + [None] * 5, [out_grad] + [None] * 5
    act[1], act[4], act[3] = send(act[0], Y1), send(act[0], Z1), send(act[0], X1)
    act[2], act[5] = send(act[1], Y3), send(act[4], Z3)
    grad[1], grad[4] = send(grad[0], Y1, act[1]), send(grad[0], Z1, act[4])
    grad[3] = send(grad[0], X1, act[3])
    grad[2], grad[5] = send(grad[1], Y3, act[2]), send(grad[4], Z3, act[5])

    def both_cores(keep, sent):
        return added(keep, swapped(sent, CORE))

    hidden, slope = hidden_of([after(act[0], grad[1], grad[4]), *act[1:]], up_weight)
    out_parts = out_parts_of(hidden, down_weight)
    grad_now = [after(grad[0], out_parts[0]), *grad[1:]]
    down_far = send(both_cores(*weight_grad("down_grad_far", far_chip, grad_now, hidden, True)), X2)
    pre_grad = pre_grad_of(grad_now, slope, down_weight)
    up_far = send(both_cores(*weight_grad("up_grad_far", far_chip, act, pre_grad, False)), X2)
    down_keep, down_send = weight_grad(
        "down_grad_own", own_chip, grad, after(hidden, pre_grad), True
    )
    up_keep, up_send = weight_grad("up_grad_own", own_chip, act, pre_grad, False)
    in_parts = in_parts_of(after(pre_grad, down_far), up_weight)

    def collected(parts):
        y = send(added(send(parts[2], Y3), parts[1]), Y1)
        z = send(added(send(parts[5], Z3), parts[4]), Z1)
        return added(parts[0], y, z, send(parts[3], X1))

    def summed(*terms):
        return total(term.astype(F32) for term in terms)

    return (
        collected(out_parts), collected(in_parts),
        summed(up_keep, swapped(up_send, CORE), up_far),
        summed(down_keep, swapped(down_send, CORE), down_far),
    )


def solution(mesh):
    in_specs = (
        P("tok", "feat"),
        P("feat", None, None, None),
        P("feat", None, None, None),
        P("tok", "feat"),
    )
    out_specs = (
        P("tok", "feat"),
        P("tok", "feat"),
        P(("feat", "tok"), None, None, None),
        P(("feat", "tok"), None, None, None),
    )
    return jax.shard_map(
        per_device, mesh=mesh, in_specs=in_specs, out_specs=out_specs, check_vma=False
    )
```

```python
import jax
import jax.numpy as jnp
from jax import lax
from jax.experimental import pallas as pl
from jax.experimental.pallas import tpu as pltpu
from jax.sharding import PartitionSpec as P

F32 = jnp.float32
BF = jnp.bfloat16
TANH_SCALE = 0.7978845608028654
BLOCK = 256
SLOTS = 6
HELD = 4
ROWS = 768

CORE, X2, X1, X3, Y1, Y3, Z1, Z3 = 1, 2, 16, 18, 4, 12, 32, 96

VMEM = pl.BlockSpec(memory_space=pltpu.VMEM)
SMEM = pl.BlockSpec(memory_space=pltpu.SMEM)
NT = (((1,), (1,)), ((), ()))
TN = (((0,), (0,)), ((), ()))


def swapped(array, mask):
    count = lax.axis_size("feat") * lax.axis_size("tok")
    return lax.ppermute(array, ("feat", "tok"), [(i, i ^ mask) for i in range(count)])


def gelu_terms(values):
    square = values * values
    half = 0.5 + 0.5 * jnp.tanh(TANH_SCALE * (values + 0.044715 * (square * values)))
    slope = TANH_SCALE + (3.0 * 0.044715 * TANH_SCALE) * square
    return values * half, half + (2.0 * values) * (half * (1.0 - half)) * slope


def matmul(a, b, dims=(((1,), (0,)), ((), ()))):
    return lax.dot_general(a, b, dims, preferred_element_type=F32)


def total(parts):
    result = None
    for part in parts:
        result = part if result is None else result + part
    return result


def columns(j):
    return pl.ds(j * BLOCK, BLOCK)


def call(body, name, operands, outs, matmuls, specs=None, scratch=()):
    return pl.pallas_call(
        body,
        in_specs=specs or [VMEM] * len(operands),
        out_specs=[VMEM] * len(outs),
        out_shape=[jax.ShapeDtypeStruct(shape, kind) for shape, kind in outs],
        scratch_shapes=list(scratch),
        compiler_params=pltpu.CompilerParams(vmem_limit_bytes=18 << 20),
        cost_estimate=pl.CostEstimate(
            flops=matmuls * 2 * ROWS * BLOCK * BLOCK, bytes_accessed=1 << 20, transcendentals=0
        ),
        name=name,
    )(*operands)


def forward(near, up, down):
    def body(*refs):
        near_refs, (up_ref, down_ref, hidden, derivative), outs = (
            refs[:SLOTS], refs[SLOTS:SLOTS + 4], refs[SLOTS + 4:]
        )
        for j in range(HELD):
            pre_act = total(matmul(near_refs[s][...], up_ref[j, s]) for s in range(SLOTS))
            result, slope = gelu_terms(pre_act)
            hidden[:, columns(j)] = result.astype(BF)
            derivative[:, columns(j)] = slope.astype(BF)
        for s in range(SLOTS):
            outs[s][...] = total(
                matmul(hidden[:, columns(j)], down_ref[j, s]) for j in range(HELD)
            ).astype(BF)

    wide, part = ((ROWS, HELD * BLOCK), BF), ((ROWS, BLOCK), BF)
    hidden, derivative, *parts = call(
        body, "forward", (*near, up, down), [wide, wide] + [part] * SLOTS, 2 * HELD * SLOTS
    )
    return hidden, derivative, parts


def backward(near, derivative, up, down):
    def body(*refs):
        near_refs, (slope, up_ref, down_ref, pre_grad), outs = (
            refs[:SLOTS], refs[SLOTS:SLOTS + 4], refs[SLOTS + 4:]
        )
        for j in range(HELD):
            hidden_grad = total(matmul(near_refs[s][...], down_ref[j, s], NT) for s in range(SLOTS))
            pre_grad[:, columns(j)] = (hidden_grad * slope[:, columns(j)].astype(F32)).astype(BF)
        for s in range(SLOTS):
            outs[s][...] = total(
                matmul(pre_grad[:, columns(j)], up_ref[j, s], NT) for j in range(HELD)
            ).astype(BF)

    wide, part = ((ROWS, HELD * BLOCK), BF), ((ROWS, BLOCK), BF)
    pre_grad, *parts = call(
        body, "backward", (*near, derivative, up, down), [wide] + [part] * SLOTS, 2 * HELD * SLOTS
    )
    return pre_grad, parts


def weight_grad(name, core, near, wide, wide_first, earlier=()):
    def body(core_ref, *refs):
        near_refs, (wide_ref, *earlier_refs), (keep, send) = (
            refs[:SLOTS], refs[SLOTS:-2], refs[-2:]
        )
        for order, out in enumerate((send, keep)):
            group = jnp.where(core_ref[0] == order, 1, 0)
            chosen = pl.ds(pl.multiple_of(group * (2 * BLOCK), 2 * BLOCK), 2 * BLOCK)
            for s in range(SLOTS):
                sides = (wide_ref[:, chosen], near_refs[s][...])
                result = matmul(*(sides if wide_first else sides[::-1]), TN)
                for j in range(2):
                    cut = slice(j * BLOCK, (j + 1) * BLOCK)
                    block = result[cut] if wide_first else result[:, cut]
                    if earlier:
                        block = block + earlier_refs[1 - order][j, s].astype(F32)
                    out[j, s] = block.astype(BF)

    shape = ((2, SLOTS, BLOCK, BLOCK), BF)
    return call(
        body, name, (core, *near, wide, *earlier), [shape, shape], HELD * SLOTS,
        specs=[SMEM] + [VMEM] * (SLOTS + 1 + len(earlier)),
    )


def added(*arrays):
    return total(a.astype(F32) for a in arrays).astype(BF)


def per_device(activations, up_weight, down_weight, out_grad):
    place = lax.axis_index("tok")
    half = place // 2
    core = (place % 2).astype(jnp.int32).reshape(1)

    up = lax.dynamic_slice_in_dim(up_weight, half * HELD, HELD)
    down = lax.dynamic_slice_in_dim(down_weight, half * HELD, HELD)

    def after(array, *before):
        return lax.optimization_barrier((array, *before))[0]

    def send(array, mask, *before):
        return swapped(after(array, *before) if before else array, mask)

    def pair(own, far):
        return jnp.concatenate([own, far])

    act, grad, act_far, grad_far = ([None] * SLOTS for _ in range(4))
    act[0], grad[0] = activations, out_grad
    act[1], act[4], act[3] = send(act[0], Y1), send(act[0], Z1), send(act[0], X1)
    grad[1], grad[4] = send(grad[0], Y1, act[1], up, down), send(grad[0], Z1, act[4], up, down)
    act_far[0] = send(act[0], X2, act[3])
    act[2], act[5] = send(act[1], Y3), send(act[4], Z3)

    grad[2], grad[5] = send(grad[1], Y3, act[2]), send(grad[4], Z3, act[5])
    act_far[1], act_far[4] = send(act_far[0], Y1, grad[1]), send(act_far[0], Z1, grad[4])
    grad_far[0] = send(grad[0], X2, act_far[0])
    near = [after(act[0], grad[1], grad[4]), *act[1:]]
    hidden, slope, out_own = forward(near, up, down)

    grad_far[1] = send(grad_far[0], Y1, act_far[1])
    grad_far[4] = send(grad_far[0], Z1, act_far[4])
    act_far[2] = send(act_far[1], Y3, grad[2])
    act_far[5] = send(act_far[4], Z3, grad[5])
    act_far[3] = send(act[0], X3, grad_far[0])

    grad_far[2] = send(grad_far[1], Y3, act_far[2])
    grad_far[5] = send(grad_far[4], Z3, act_far[5])
    grad[3] = send(grad[0], X1, act_far[3])
    near = [after(act_far[0], grad_far[1], grad_far[4]), *act_far[1:]]
    hidden_far, slope_far, out_far = forward(near, up, down)

    out_y = send(pair(out_own[2], out_far[2]), Y3, grad_far[2])
    out_z = send(pair(out_own[5], out_far[5]), Z3, grad_far[5])
    grad_far[3] = send(grad[0], X3, grad[3])
    pre_grad, in_own = backward(grad, slope, up, down)
    down_own = weight_grad("down_weight_grad", core, grad, after(hidden, in_own[0]), True)
    pre_grad_far, in_far = backward(grad_far, after(slope_far, down_own[0]), up, down)

    x_out_own, x_out_far = send(out_own[3], X1, grad[3]), send(out_far[3], X3, grad_far[3])
    x_in_own = send(in_own[3], X1, x_out_own)
    in_y = send(pair(in_own[2], in_far[2]), Y3, out_y, x_in_own, x_out_far)
    in_z = send(pair(in_own[5], in_far[5]), Z3, out_z, x_in_own, x_out_far)
    down_keep, down_send = weight_grad(
        "down_weight_grad", core, grad_far, after(hidden_far, out_y, out_z), True, down_own
    )
    out_y = send(added(out_y, pair(out_own[1], out_far[1])), Y1)
    out_z = send(added(out_z, pair(out_own[4], out_far[4])), Z1)
    x_in_far = send(in_far[3], X3, down_keep)
    up_own = weight_grad("up_weight_grad", core, act, after(pre_grad, down_keep), False)
    up_keep, up_send = weight_grad(
        "up_weight_grad", core, act_far, after(pre_grad_far, in_y, in_z, out_y, out_z, x_in_far), False, up_own
    )

    in_far_y = send(added(in_y[ROWS:], in_far[1]), Y1, out_y)
    in_far_z = send(added(in_z[ROWS:], in_far[4]), Z1, out_z)
    in_own_y = send(added(in_y[:ROWS], in_own[1]), Y1, in_far_y)
    in_own_z = send(added(in_z[:ROWS], in_own[4]), Z1, in_far_z)
    out_home = send(added(out_far[0], out_y[ROWS:], out_z[ROWS:]), X2)
    in_home = send(added(in_far[0], in_far_y, in_far_z), X2, out_home)
    down_other = swapped(down_send, CORE)
    up_other = send(up_send, CORE, out_home)
    output = added(out_own[0], out_y[:ROWS], out_z[:ROWS], x_out_own, x_out_far, out_home)
    in_grad = added(in_own[0], in_own_y, in_own_z, x_in_own, x_in_far, in_home)
    down_grad = down_keep.astype(F32) + down_other.astype(F32)
    up_grad = up_keep.astype(F32) + up_other.astype(F32)
    return output, in_grad, up_grad, down_grad


def solution(mesh):
    in_specs = (
        P("tok", "feat"),
        P("feat", None, None, None),
        P("feat", None, None, None),
        P("tok", "feat"),
    )
    out_specs = (
        P("tok", "feat"),
        P("tok", "feat"),
        P(("feat", "tok"), None, None, None),
        P(("feat", "tok"), None, None, None),
    )
    return jax.shard_map(
        per_device, mesh=mesh, in_specs=in_specs, out_specs=out_specs, check_vma=False
    )
```

```python
import jax
import jax.numpy as jnp
from jax import lax
from jax.experimental import pallas as pl
from jax.experimental.pallas import tpu as pltpu
from jax.sharding import PartitionSpec as P

F32 = jnp.float32
BF = jnp.bfloat16
TANH_SCALE = 0.7978845608028654
BLOCK = 256
SLOTS = 6
HELD = 4
ROWS = 768

CORE, X2, X1, X3, Y1, Y3, Z1, Z3 = 1, 2, 16, 18, 4, 12, 32, 96

VMEM = pl.BlockSpec(memory_space=pltpu.VMEM)
SMEM = pl.BlockSpec(memory_space=pltpu.SMEM)
NT = (((1,), (1,)), ((), ()))
TN = (((0,), (0,)), ((), ()))


def swapped(array, mask):
    count = lax.axis_size("feat") * lax.axis_size("tok")
    return lax.ppermute(array, ("feat", "tok"), [(i, i ^ mask) for i in range(count)])


def gelu_terms(values):
    square = values * values
    half = 0.5 + 0.5 * jnp.tanh(TANH_SCALE * (values + 0.044715 * (square * values)))
    slope = TANH_SCALE + (3.0 * 0.044715 * TANH_SCALE) * square
    return values * half, half + (2.0 * values) * (half * (1.0 - half)) * slope


def matmul(a, b, dims=(((1,), (0,)), ((), ()))):
    return lax.dot_general(a, b, dims, preferred_element_type=F32)


def total(parts):
    result = None
    for part in parts:
        result = part if result is None else result + part
    return result


def columns(j):
    return pl.ds(j * BLOCK, BLOCK)


def call(body, name, operands, outs, matmuls, specs=None, scratch=()):
    return pl.pallas_call(
        body,
        in_specs=specs or [VMEM] * len(operands),
        out_specs=[VMEM] * len(outs),
        out_shape=[jax.ShapeDtypeStruct(shape, kind) for shape, kind in outs],
        scratch_shapes=list(scratch),
        compiler_params=pltpu.CompilerParams(vmem_limit_bytes=18 << 20),
        cost_estimate=pl.CostEstimate(
            flops=matmuls * 2 * ROWS * BLOCK * BLOCK, bytes_accessed=1 << 20, transcendentals=0
        ),
        name=name,
    )(*operands)


def forward(near, up, down):
    def body(*refs):
        near_refs, (up_ref, down_ref, hidden, derivative), outs = (
            refs[:SLOTS], refs[SLOTS:SLOTS + 4], refs[SLOTS + 4:]
        )
        for j in range(HELD):
            pre_act = total(matmul(near_refs[s][...], up_ref[j, s]) for s in range(SLOTS))
            result, slope = gelu_terms(pre_act)
            hidden[:, columns(j)] = result.astype(BF)
            derivative[:, columns(j)] = slope.astype(BF)
        for s in range(SLOTS):
            outs[s][...] = total(
                matmul(hidden[:, columns(j)], down_ref[j, s]) for j in range(HELD)
            ).astype(BF)

    wide, part = ((ROWS, HELD * BLOCK), BF), ((ROWS, BLOCK), BF)
    hidden, derivative, *parts = call(
        body, "forward", (*near, up, down), [wide, wide] + [part] * SLOTS, 2 * HELD * SLOTS
    )
    return hidden, derivative, parts


def backward(near, derivative, up, down):
    def body(*refs):
        near_refs, (slope, up_ref, down_ref, pre_grad), outs = (
            refs[:SLOTS], refs[SLOTS:SLOTS + 4], refs[SLOTS + 4:]
        )
        for j in range(HELD):
            hidden_grad = total(matmul(near_refs[s][...], down_ref[j, s], NT) for s in range(SLOTS))
            pre_grad[:, columns(j)] = (hidden_grad * slope[:, columns(j)].astype(F32)).astype(BF)
        for s in range(SLOTS):
            outs[s][...] = total(
                matmul(pre_grad[:, columns(j)], up_ref[j, s], NT) for j in range(HELD)
            ).astype(BF)

    wide, part = ((ROWS, HELD * BLOCK), BF), ((ROWS, BLOCK), BF)
    pre_grad, *parts = call(
        body, "backward", (*near, derivative, up, down), [wide] + [part] * SLOTS, 2 * HELD * SLOTS
    )
    return pre_grad, parts


def weight_grad(name, core, near, wide, wide_first, earlier=()):
    def body(core_ref, *refs):
        near_refs, (wide_ref, *earlier_refs), (keep, send) = (
            refs[:SLOTS], refs[SLOTS:-2], refs[-2:]
        )
        for order, out in enumerate((send, keep)):
            group = jnp.where(core_ref[0] == order, 1, 0)
            chosen = pl.ds(pl.multiple_of(group * (2 * BLOCK), 2 * BLOCK), 2 * BLOCK)
            for s in range(SLOTS):
                sides = (wide_ref[:, chosen], near_refs[s][...])
                result = matmul(*(sides if wide_first else sides[::-1]), TN)
                for j in range(2):
                    cut = slice(j * BLOCK, (j + 1) * BLOCK)
                    block = result[cut] if wide_first else result[:, cut]
                    if earlier:
                        block = block + earlier_refs[1 - order][j, s].astype(F32)
                    out[j, s] = block.astype(BF)

    shape = ((2, SLOTS, BLOCK, BLOCK), BF)
    return call(
        body, name, (core, *near, wide, *earlier), [shape, shape], HELD * SLOTS,
        specs=[SMEM] + [VMEM] * (SLOTS + 1 + len(earlier)),
    )


def added(*arrays):
    return total(a.astype(F32) for a in arrays).astype(BF)


def per_device(activations, up_weight, down_weight, out_grad):
    place = lax.axis_index("tok")
    half = place // 2
    core = (place % 2).astype(jnp.int32).reshape(1)

    up = lax.dynamic_slice_in_dim(up_weight, half * HELD, HELD)
    down = lax.dynamic_slice_in_dim(down_weight, half * HELD, HELD)

    def after(array, *before):
        return lax.optimization_barrier((array, *before))[0]

    def send(array, mask, *before):
        return swapped(after(array, *before) if before else array, mask)

    def pair(own, far):
        return jnp.concatenate([own, far])

    act, grad, act_far, grad_far = ([None] * SLOTS for _ in range(4))
    act[0], grad[0] = activations, out_grad
    act[1], act[4], act[3] = send(act[0], Y1), send(act[0], Z1), send(act[0], X1)
    grad[1], grad[4] = send(grad[0], Y1, act[1], up, down), send(grad[0], Z1, act[4], up, down)
    act_far[0] = send(act[0], X2, act[3])
    act[2], act[5] = send(act[1], Y3), send(act[4], Z3)

    grad[2], grad[5] = send(grad[1], Y3, act[2]), send(grad[4], Z3, act[5])
    act_far[1], act_far[4] = send(act_far[0], Y1, grad[1]), send(act_far[0], Z1, grad[4])
    grad_far[0] = send(grad[0], X2, act_far[0])
    near = [after(act[0], grad[1], grad[4]), *act[1:]]
    hidden, slope, out_own = forward(near, up, down)

    grad_far[1] = send(grad_far[0], Y1, act_far[1])
    grad_far[4] = send(grad_far[0], Z1, act_far[4])
    act_far[2] = send(act_far[1], Y3, grad[2])
    act_far[5] = send(act_far[4], Z3, grad[5])
    act_far[3] = send(act[0], X3, grad_far[0])

    grad_far[2] = send(grad_far[1], Y3, act_far[2])
    grad_far[5] = send(grad_far[4], Z3, act_far[5])
    grad[3] = send(grad[0], X1, act_far[3])
    near = [after(act_far[0], grad_far[1], grad_far[4]), *act_far[1:]]
    hidden_far, slope_far, out_far = forward(near, up, down)

    out_y = send(pair(out_own[2], out_far[2]), Y3, grad_far[2])
    out_z = send(pair(out_own[5], out_far[5]), Z3, grad_far[5])
    grad_far[3] = send(grad[0], X3, grad[3])
    pre_grad, in_own = backward(grad, slope, up, down)
    down_own = weight_grad("down_weight_grad", core, grad, after(hidden, in_own[0]), True)
    pre_grad_far, in_far = backward(grad_far, after(slope_far, down_own[0]), up, down)

    x_out_own, x_out_far = send(out_own[3], X1, grad[3]), send(out_far[3], X3, grad_far[3])
    x_in_own = send(in_own[3], X1, x_out_own)
    in_y = send(pair(in_own[2], in_far[2]), Y3, out_y, x_in_own, x_out_far)
    in_z = send(pair(in_own[5], in_far[5]), Z3, out_z, x_in_own, x_out_far)
    down_keep, down_send = weight_grad(
        "down_weight_grad", core, grad_far, after(hidden_far, out_y, out_z), True, down_own
    )
    out_y = send(added(out_y, pair(out_own[1], out_far[1])), Y1)
    out_z = send(added(out_z, pair(out_own[4], out_far[4])), Z1)
    x_in_far = send(in_far[3], X3, down_keep)
    up_own = weight_grad("up_weight_grad", core, act, after(pre_grad, down_keep), False)
    up_keep, up_send = weight_grad(
        "up_weight_grad", core, act_far, after(pre_grad_far, in_y, in_z, out_y, out_z, x_in_far), False, up_own
    )

    in_far_y = send(added(in_y[ROWS:], in_far[1]), Y1, out_y, up_own[0])
    in_far_z = send(added(in_z[ROWS:], in_far[4]), Z1, out_z, up_own[0])
    in_own_y = send(added(in_y[:ROWS], in_own[1]), Y1, in_far_y)
    in_own_z = send(added(in_z[:ROWS], in_own[4]), Z1, in_far_z)
    out_home = send(added(out_far[0], out_y[ROWS:], out_z[ROWS:]), X2)
    in_home = send(added(in_far[0], in_far_y, in_far_z), X2, out_home)
    down_other = swapped(down_send, CORE)
    up_other = send(up_send, CORE, out_home, in_far_y, in_far_z)
    output = added(out_own[0], out_y[:ROWS], out_z[:ROWS], x_out_own, x_out_far, out_home)
    down_grad = down_keep.astype(F32) + down_other.astype(F32)
    up_grad = up_keep.astype(F32) + up_other.astype(F32)
    in_grad = added(after(in_own[0], up_grad), in_own_y, in_own_z, x_in_own, x_in_far, in_home)
    return output, in_grad, up_grad, down_grad


def solution(mesh):
    in_specs = (
        P("tok", "feat"),
        P("feat", None, None, None),
        P("feat", None, None, None),
        P("tok", "feat"),
    )
    out_specs = (
        P("tok", "feat"),
        P("tok", "feat"),
        P(("feat", "tok"), None, None, None),
        P(("feat", "tok"), None, None, None),
    )
    return jax.shard_map(
        per_device, mesh=mesh, in_specs=in_specs, out_specs=out_specs, check_vma=False
    )
```

```python
import jax
import jax.numpy as jnp
from jax import lax
from jax.experimental import pallas as pl
from jax.experimental.pallas import tpu as pltpu
from jax.sharding import PartitionSpec as P

F32 = jnp.float32
BF = jnp.bfloat16
TANH_SCALE = 0.7978845608028654
BLOCK = 256
SLOTS = 6
HELD = 4
ROWS = 768

CORE, X2, X1, X3, Y1, Y3, Z1, Z3 = 1, 2, 16, 18, 4, 12, 32, 96

VMEM = pl.BlockSpec(memory_space=pltpu.VMEM)
SMEM = pl.BlockSpec(memory_space=pltpu.SMEM)
NT = (((1,), (1,)), ((), ()))
TN = (((0,), (0,)), ((), ()))


def swapped(array, mask):
    count = lax.axis_size("feat") * lax.axis_size("tok")
    return lax.ppermute(array, ("feat", "tok"), [(i, i ^ mask) for i in range(count)])


def gelu_terms(values):
    square = values * values
    half = 0.5 + 0.5 * jnp.tanh(TANH_SCALE * (values + 0.044715 * (square * values)))
    slope = TANH_SCALE + (3.0 * 0.044715 * TANH_SCALE) * square
    return values * half, half + (2.0 * values) * (half * (1.0 - half)) * slope


def matmul(a, b, dims=(((1,), (0,)), ((), ()))):
    return lax.dot_general(a, b, dims, preferred_element_type=F32)


def total(parts):
    result = None
    for part in parts:
        result = part if result is None else result + part
    return result


def columns(j):
    return pl.ds(j * BLOCK, BLOCK)


def call(body, name, operands, outs, matmuls, specs=None, scratch=()):
    return pl.pallas_call(
        body,
        in_specs=specs or [VMEM] * len(operands),
        out_specs=[VMEM] * len(outs),
        out_shape=[jax.ShapeDtypeStruct(shape, kind) for shape, kind in outs],
        scratch_shapes=list(scratch),
        compiler_params=pltpu.CompilerParams(vmem_limit_bytes=18 << 20),
        cost_estimate=pl.CostEstimate(
            flops=matmuls * 2 * ROWS * BLOCK * BLOCK, bytes_accessed=1 << 20, transcendentals=0
        ),
        name=name,
    )(*operands)


def forward(near, up, down):
    def body(*refs):
        near_refs, (up_ref, down_ref, hidden, derivative), outs = (
            refs[:SLOTS], refs[SLOTS:SLOTS + 4], refs[SLOTS + 4:]
        )
        @pl.loop(0, HELD)
        def _(j):
            pre_act = total(matmul(near_refs[s][...], up_ref[j, s]) for s in range(SLOTS))
            result, slope = gelu_terms(pre_act)
            place = pl.ds(pl.multiple_of(j * BLOCK, BLOCK), BLOCK)
            hidden[:, place] = result.astype(BF)
            derivative[:, place] = slope.astype(BF)

        for s in range(SLOTS):
            outs[s][...] = total(
                matmul(hidden[:, columns(j)], down_ref[j, s]) for j in range(HELD)
            ).astype(BF)

    wide, part = ((ROWS, HELD * BLOCK), BF), ((ROWS, BLOCK), BF)
    hidden, derivative, *parts = call(
        body, "forward", (*near, up, down), [wide, wide] + [part] * SLOTS, 2 * HELD * SLOTS
    )
    return hidden, derivative, parts


def backward(near, derivative, up, down):
    def body(*refs):
        near_refs, (slope, up_ref, down_ref, pre_grad), outs = (
            refs[:SLOTS], refs[SLOTS:SLOTS + 4], refs[SLOTS + 4:]
        )
        @pl.loop(0, HELD)
        def _(j):
            hidden_grad = total(matmul(near_refs[s][...], down_ref[j, s], NT) for s in range(SLOTS))
            place = pl.ds(pl.multiple_of(j * BLOCK, BLOCK), BLOCK)
            pre_grad[:, place] = (hidden_grad * slope[:, place].astype(F32)).astype(BF)

        for s in range(SLOTS):
            outs[s][...] = total(
                matmul(pre_grad[:, columns(j)], up_ref[j, s], NT) for j in range(HELD)
            ).astype(BF)

    wide, part = ((ROWS, HELD * BLOCK), BF), ((ROWS, BLOCK), BF)
    pre_grad, *parts = call(
        body, "backward", (*near, derivative, up, down), [wide] + [part] * SLOTS, 2 * HELD * SLOTS
    )
    return pre_grad, parts


def weight_grad(name, core, near, wide, wide_first, earlier=()):
    def body(core_ref, *refs):
        near_refs, (wide_ref, *earlier_refs), (keep, send) = (
            refs[:SLOTS], refs[SLOTS:-2], refs[-2:]
        )
        for order, out in enumerate((send, keep)):
            group = jnp.where(core_ref[0] == order, 1, 0)
            chosen = pl.ds(pl.multiple_of(group * (2 * BLOCK), 2 * BLOCK), 2 * BLOCK)
            for s in range(SLOTS):
                sides = (wide_ref[:, chosen], near_refs[s][...])
                result = matmul(*(sides if wide_first else sides[::-1]), TN)
                for j in range(2):
                    cut = slice(j * BLOCK, (j + 1) * BLOCK)
                    block = result[cut] if wide_first else result[:, cut]
                    if earlier:
                        block = block + earlier_refs[1 - order][j, s].astype(F32)
                    out[j, s] = block.astype(BF)

    shape = ((2, SLOTS, BLOCK, BLOCK), BF)
    return call(
        body, name, (core, *near, wide, *earlier), [shape, shape], HELD * SLOTS,
        specs=[SMEM] + [VMEM] * (SLOTS + 1 + len(earlier)),
    )


def added(*arrays):
    return total(a.astype(F32) for a in arrays).astype(BF)


def per_device(activations, up_weight, down_weight, out_grad):
    place = lax.axis_index("tok")
    half = place // 2
    core = (place % 2).astype(jnp.int32).reshape(1)

    up = lax.dynamic_slice_in_dim(up_weight, half * HELD, HELD)
    down = lax.dynamic_slice_in_dim(down_weight, half * HELD, HELD)

    def after(array, *before):
        return lax.optimization_barrier((array, *before))[0]

    def send(array, mask, *before):
        return swapped(after(array, *before) if before else array, mask)

    def pair(own, far):
        return jnp.concatenate([own, far])

    act, grad, act_far, grad_far = ([None] * SLOTS for _ in range(4))
    act[0], grad[0] = activations, out_grad
    act[1], act[4], act[3] = send(act[0], Y1), send(act[0], Z1), send(act[0], X1)
    grad[1], grad[4] = send(grad[0], Y1, act[1], up, down), send(grad[0], Z1, act[4], up, down)
    act_far[0] = send(act[0], X2, act[3])
    act[2], act[5] = send(act[1], Y3), send(act[4], Z3)

    grad[2], grad[5] = send(grad[1], Y3, act[2]), send(grad[4], Z3, act[5])
    act_far[1], act_far[4] = send(act_far[0], Y1, grad[1]), send(act_far[0], Z1, grad[4])
    grad_far[0] = send(grad[0], X2, act_far[0])
    near = [after(act[0], grad[1], grad[4]), *act[1:]]
    hidden, slope, out_own = forward(near, up, down)

    grad_far[1] = send(grad_far[0], Y1, act_far[1])
    grad_far[4] = send(grad_far[0], Z1, act_far[4])
    act_far[2] = send(act_far[1], Y3, grad[2])
    act_far[5] = send(act_far[4], Z3, grad[5])
    act_far[3] = send(act[0], X3, grad_far[0])

    grad_far[2] = send(grad_far[1], Y3, act_far[2])
    grad_far[5] = send(grad_far[4], Z3, act_far[5])
    grad[3] = send(grad[0], X1, act_far[3])
    near = [after(act_far[0], grad_far[1], grad_far[4]), *act_far[1:]]
    hidden_far, slope_far, out_far = forward(near, up, down)

    out_y = send(pair(out_own[2], out_far[2]), Y3, grad_far[2])
    out_z = send(pair(out_own[5], out_far[5]), Z3, grad_far[5])
    grad_far[3] = send(grad[0], X3, grad[3])
    pre_grad, in_own = backward(grad, slope, up, down)
    down_own = weight_grad("down_weight_grad", core, grad, after(hidden, in_own[0]), True)
    pre_grad_far, in_far = backward(grad_far, after(slope_far, down_own[0]), up, down)

    x_out_own, x_out_far = send(out_own[3], X1, grad[3]), send(out_far[3], X3, grad_far[3])
    x_in_own = send(in_own[3], X1, x_out_own)
    in_y = send(pair(in_own[2], in_far[2]), Y3, out_y, x_in_own, x_out_far)
    in_z = send(pair(in_own[5], in_far[5]), Z3, out_z, x_in_own, x_out_far)
    down_keep, down_send = weight_grad(
        "down_weight_grad", core, grad_far, after(hidden_far, out_y, out_z), True, down_own
    )
    out_y = send(added(out_y, pair(out_own[1], out_far[1])), Y1)
    out_z = send(added(out_z, pair(out_own[4], out_far[4])), Z1)
    x_in_far = send(in_far[3], X3, down_keep)
    up_own = weight_grad("up_weight_grad", core, act, after(pre_grad, down_keep), False)
    up_keep, up_send = weight_grad(
        "up_weight_grad", core, act_far, after(pre_grad_far, in_y, in_z, out_y, out_z, x_in_far), False, up_own
    )

    in_far_y = send(added(in_y[ROWS:], in_far[1]), Y1, out_y)
    in_far_z = send(added(in_z[ROWS:], in_far[4]), Z1, out_z)
    in_own_y = send(added(in_y[:ROWS], in_own[1]), Y1, in_far_y)
    in_own_z = send(added(in_z[:ROWS], in_own[4]), Z1, in_far_z)
    out_home = send(added(out_far[0], out_y[ROWS:], out_z[ROWS:]), X2)
    in_home = send(added(in_far[0], in_far_y, in_far_z), X2, out_home)
    down_other = swapped(down_send, CORE)
    up_other = send(up_send, CORE, out_home)
    output = added(out_own[0], out_y[:ROWS], out_z[:ROWS], x_out_own, x_out_far, out_home)
    in_grad = added(in_own[0], in_own_y, in_own_z, x_in_own, x_in_far, in_home)
    down_grad = down_keep.astype(F32) + down_other.astype(F32)
    up_grad = up_keep.astype(F32) + up_other.astype(F32)
    return output, in_grad, up_grad, down_grad


def solution(mesh):
    in_specs = (
        P("tok", "feat"),
        P("feat", None, None, None),
        P("feat", None, None, None),
        P("tok", "feat"),
    )
    out_specs = (
        P("tok", "feat"),
        P("tok", "feat"),
        P(("feat", "tok"), None, None, None),
        P(("feat", "tok"), None, None, None),
    )
    return jax.shard_map(
        per_device, mesh=mesh, in_specs=in_specs, out_specs=out_specs, check_vma=False
    )
```
